32 devices in a mesh: row: 8 (over y, x, core), col: 4 (over z).
Axes of the slice: x: 2, y: 2, z: 4, core: 2. Of those that a mesh axis runs over, the one named last changes fastest.
Arguments:
- activations: bfloat16 [256, 16384], P('col', 'row'), may hold values from -6 to 6
- grad_out: bfloat16 [256, 16384], P('col', 'row'), may hold values from -1.5 to 1.5
- first_blocks: bfloat16 [8, 4, 384, 128, 128], P('row', 'col'), may hold values from -0.125 to 0.125
- first_coords: int32 [8, 4, 384, 2], P('row', 'col'), may hold values from -1 to 511, as said below
- second_blocks: bfloat16 [4, 8, 384, 128, 128], P('col', 'row'), may hold values from -0.0625 to 0.0625
- second_coords: int32 [4, 8, 384, 2], P('col', 'row'), may hold values from -1 to 511, as said below
Outputs:
- output: float32 [256, 16384], P('col', 'row')
- grad_input: float32 [256, 16384], P('col', 'row')
- grad_first: bfloat16 [8, 4, 384, 128, 128], P('row', 'col')
- grad_second: bfloat16 [4, 8, 384, 128, 128], P('col', 'row')
The draws below stay inside these ranges and needn't reach their ends.
Inputs may be any that keep to these rules, and one draw needn't show every extreme that they name: `first_coords`: tile [a, b] lists, once each, exactly the nonzero blocks of W1 whose block row lies in a * 16 to a * 16 + 15 and whose block column lies in b * 128 to b * 128 + 127, in increasing order of block row and then block column; the remaining of its 384 slots hold -1 in both coordinates. Some tile fills all 384 slots. `second_coords`: tile [a, b] lists, once each, exactly the nonzero blocks of W2 whose block row lies in a * 128 to a * 128 + 127 and whose block column lies in b * 16 to b * 16 + 15, in increasing order of block row and then block column; the remaining of its 384 slots hold -1 in both coordinates. Some tile fills all 384 slots.
All inputs are finite; a program needn't handle non-finite values.
Results may differ from the reference program's by a relative error of at most 0.005.
Values may be sent and summed in bfloat16 or wider, within the bound.
A program may use at most 320 MiB of HBM per device.

```python
import jax
import jax.numpy as jnp
from jax import lax

D = 16384
FF = 65536
BLK = 128
TOKENS = 256
DB = 128
FB = 512
RB = 16
CB = 128
CAP = 384
N_ROW = 8
N_COL = 4


def single_bit(values):
    return jnp.bitwise_and(values, values - 1) == 0


def butterfly_pattern(key, rows_total, cols_total, rows_tile, cols_tile, rows_model):
    model_xor = jax.random.randint(jax.random.fold_in(key, 1), (), 0, DB, dtype=jnp.int32)
    hidden_xor = jax.random.randint(jax.random.fold_in(key, 2), (), 0, FB, dtype=jnp.int32)
    group_count = FB // CB
    group_table = jax.random.randint(jax.random.fold_in(key, 3), (group_count,), 0, DB, dtype=jnp.int32)
    row_groups = rows_total // rows_tile
    col_groups = cols_total // cols_tile
    full_shape = (row_groups, col_groups, rows_tile, cols_tile)
    grid_rows = jnp.broadcast_to(jnp.arange(row_groups, dtype=jnp.int32)[:, None, None, None] * rows_tile + jnp.arange(rows_tile, dtype=jnp.int32)[None, None, :, None], full_shape)
    grid_cols = jnp.broadcast_to(jnp.arange(col_groups, dtype=jnp.int32)[None, :, None, None] * cols_tile + jnp.arange(cols_tile, dtype=jnp.int32)[None, None, None, :], full_shape)
    if rows_model:
        model_index, hidden_index = (grid_rows, grid_cols)
    else:
        model_index, hidden_index = (grid_cols, grid_rows)
    group_xor = jnp.take(group_table, hidden_index // CB)
    offset = jnp.right_shift(jnp.bitwise_xor(hidden_index, hidden_xor), 2)
    differ = jnp.bitwise_xor(offset, jnp.bitwise_xor(model_index, jnp.bitwise_xor(model_xor, group_xor)))
    nonzero = single_bit(differ) | single_bit(jnp.bitwise_xor(differ, DB - 1))
    tile_span = rows_tile * cols_tile
    nonzero_flags = nonzero.reshape(row_groups, col_groups, tile_span).astype(jnp.int32)
    scores = (1 - nonzero_flags) * tile_span + jnp.arange(tile_span, dtype=jnp.int32)
    ranking = jnp.argsort(scores, axis=-1)[..., :CAP]
    is_kept = jnp.take_along_axis(nonzero_flags, ranking, axis=-1) > 0
    rows_flat = jnp.take_along_axis(grid_rows.reshape(row_groups, col_groups, tile_span), ranking, axis=-1)
    cols_flat = jnp.take_along_axis(grid_cols.reshape(row_groups, col_groups, tile_span), ranking, axis=-1)
    coords = jnp.stack([jnp.where(is_kept, rows_flat, -1), jnp.where(is_kept, cols_flat, -1)], axis=-1)
    return coords.astype(jnp.int32)


def draw_first_coords(key, part):
    return butterfly_pattern(jax.random.fold_in(key, 101), DB, FB, RB, CB, True)


def draw_second_coords(key, part):
    return butterfly_pattern(jax.random.fold_in(key, 202), FB, DB, CB, RB, False)


def shard_levels(key, shape, split, low, top_value):
    factor_of = 1.0
    for position, blocks in split:
        draws = jax.random.uniform(jax.random.fold_in(jax.random.fold_in(key, 6), position), (blocks,), jnp.float32, low / len(split), top_value / len(split))
        factor_of = factor_of * jnp.repeat(jnp.exp(draws), shape[position] // blocks).reshape((-1,) + (1,) * (len(shape) - 1 - position))
    return factor_of


def gaussian(key, extent, deviation, reach, shards=(), kind=jnp.bfloat16):
    values = jax.random.normal(key, extent, jnp.float32) * deviation
    if len(shards) > 0:
        values = shard_levels(key, extent, shards, -0.22, 0.18) * values
    return jnp.clip(values, min=-reach, max=reach).astype(kind)


def setup_inputs(seed: int = 0) -> dict:
    arg_keys = jax.random.split(jax.random.key(seed), 7)
    activations = gaussian(arg_keys[0], (TOKENS, D), 1.0, 6.0, ((0, 4), (1, 8)))
    grad_out = gaussian(arg_keys[1], (TOKENS, D), 0.25, 1.5, ((0, 4), (1, 8)))
    first_blocks = gaussian(arg_keys[2], (N_ROW, N_COL, CAP, BLK, BLK), (D // 8) ** -0.5, 0.125, ((0, 8), (1, 4)))
    first_coords = draw_first_coords(jax.random.fold_in(arg_keys[6], 71), 0)
    second_blocks = gaussian(arg_keys[4], (N_COL, N_ROW, CAP, BLK, BLK), (FF // 8) ** -0.5, 0.0625, ((0, 4), (1, 8)))
    second_coords = draw_second_coords(jax.random.fold_in(arg_keys[6], 71), 0)
    return dict(activations=activations, grad_out=grad_out, first_blocks=first_blocks, first_coords=first_coords, second_blocks=second_blocks, second_coords=second_coords)


def gelu_tanh(values):
    return jax.nn.gelu(values, approximate=True)

def tile_product(panels, blocks, coords, source_axis, target_axis, segments, flipped):
    token_count = panels.shape[0]
    block_grid = panels.reshape(token_count, -1, BLK)
    flat_blocks = blocks.reshape(-1, CAP, BLK, BLK)
    flat_coords = coords.reshape(-1, CAP, 2)

    def advance(totals, member):
        tile_blocks, tile_coords = member
        is_live = tile_coords[:, 0] >= 0
        source = jnp.where(is_live, tile_coords[:, source_axis], 0).astype(jnp.int32)
        target = jnp.where(is_live, tile_coords[:, target_axis], segments).astype(jnp.int32)
        picked = jnp.take(block_grid, source, axis=1).astype(jnp.float32)
        weights = tile_blocks.astype(jnp.float32)
        if flipped:
            products = jnp.einsum('rsk,snk->srn', picked, weights)
        else:
            products = jnp.einsum('rsk,skn->srn', picked, weights)
        return (totals.at[target].add(products), None)
    initial = jnp.zeros((segments + 1, token_count, BLK), jnp.float32)
    totals, unused = lax.scan(advance, initial, (flat_blocks, flat_coords))
    return jnp.transpose(totals[:segments], (1, 0, 2)).reshape(token_count, segments * BLK)

def tile_grads(left, right, coords, blocks_shape):
    token_count = left.shape[0]
    left_grid = left.reshape(token_count, -1, BLK)
    right_grid = right.reshape(token_count, -1, BLK)
    flat_coords = coords.reshape(-1, CAP, 2)

    def advance(carry, tile_coords):
        is_live = tile_coords[:, 0] >= 0
        left_source = jnp.where(is_live, tile_coords[:, 0], 0).astype(jnp.int32)
        right_source = jnp.where(is_live, tile_coords[:, 1], 0).astype(jnp.int32)
        picked_left = jnp.take(left_grid, left_source, axis=1).astype(jnp.float32)
        picked_right = jnp.take(right_grid, right_source, axis=1).astype(jnp.float32)
        grads = jnp.einsum('rsk,rsn->skn', picked_left, picked_right)
        grads = jnp.where(is_live[:, None, None], grads, jnp.float32(0.0)).astype(jnp.bfloat16)
        return (carry, grads)
    unused, stacked = lax.scan(advance, jnp.zeros((), jnp.float32), flat_coords)
    return stacked.reshape(blocks_shape)

def reference(activations, grad_out, first_blocks, first_coords, second_blocks, second_coords):
    pre = tile_product(activations, first_blocks, first_coords, 0, 1, FB, False)
    hidden_full, gelu_back = jax.vjp(gelu_tanh, pre)
    hidden = hidden_full.astype(jnp.bfloat16)
    output = tile_product(hidden, second_blocks, second_coords, 0, 1, DB, False)
    grad_hidden = tile_product(grad_out, second_blocks, second_coords, 1, 0, FB, True)
    grad_pre = gelu_back(grad_hidden)[0].astype(jnp.bfloat16)
    grad_input = tile_product(grad_pre, first_blocks, first_coords, 1, 0, DB, True)
    grad_first = tile_grads(activations, grad_pre, first_coords, first_blocks.shape)
    grad_second = tile_grads(hidden, grad_out, second_coords, second_blocks.shape)
    return (output, grad_input, grad_first, grad_second)
```

```python
import functools
import math

import jax
import jax.numpy as jnp
from jax import lax
from jax.experimental import pallas as pl
from jax.experimental.pallas import tpu as pltpu
from jax.sharding import PartitionSpec as P

FF = 65536
CHUNK = 32
VMEM_LIMIT = 58 * 1024 * 1024


def gelu_tanh(values):
    return jax.nn.gelu(values, approximate=True)


def contract(left, right, left_dim, right_dim):
    return lax.dot_general(
        left, right, (((left_dim,), (right_dim,)), ((), ())), preferred_element_type=jnp.float32
    )


def lanes(ref, index, width):
    return ref[:, pl.ds(pl.multiple_of(index * width, width), width)]


def to_hidden_kernel(flipped, source, target, panel, weights, keep, send, totals):
    step = pl.program_id(0)
    segments = totals.shape[0] - 1
    half = segments // 2
    width = weights.shape[-1]

    @pl.when(step == 0)
    def _():
        def clear(index, carry):
            totals[index] = jnp.zeros(totals.shape[1:], jnp.float32)
            return carry

        lax.fori_loop(0, segments, clear, 0)

    for slot in range(CHUNK):
        k = step * CHUNK + slot
        term = contract(
            lanes(panel, source[k], width), weights[slot], 1, 1 if flipped else 0
        )
        totals[target[k]] += term

    @pl.when(step == pl.num_programs(0) - 1)
    def _():
        def write(index, carry):
            keep[index] = totals[index]
            send[index] = totals[half + index].astype(jnp.bfloat16)
            return carry

        lax.fori_loop(0, half, write, 0)


def to_hidden(panel, weights, source, target, segments, flipped):
    tokens = panel.shape[0]
    slots, width, _ = weights.shape
    half = segments // 2
    return pl.pallas_call(
        functools.partial(to_hidden_kernel, flipped),
        grid_spec=pltpu.PrefetchScalarGridSpec(
            num_scalar_prefetch=2,
            grid=(slots // CHUNK,),
            in_specs=[
                pl.BlockSpec(panel.shape, lambda s, a, b: (0, 0)),
                pl.BlockSpec((CHUNK, width, width), lambda s, a, b: (s, 0, 0)),
            ],
            out_specs=[pl.BlockSpec((half, tokens, width), lambda s, a, b: (0, 0, 0))] * 2,
            scratch_shapes=[pltpu.VMEM((segments + 1, tokens, width), jnp.float32)],
        ),
        out_shape=[
            jax.ShapeDtypeStruct((half, tokens, width), jnp.float32),
            jax.ShapeDtypeStruct((half, tokens, width), jnp.bfloat16),
        ],
        compiler_params=pltpu.CompilerParams(vmem_limit_bytes=VMEM_LIMIT),
        cost_estimate=pl.CostEstimate(
            flops=8 * slots * tokens * width * width,
            bytes_accessed=2 * weights.size + 6 * half * tokens * width,
            transcendentals=0,
        ),
    )(source, target, panel, weights)


def to_model_kernel(transposed, pieces, model_at, hidden_at, live, panel, weights, *refs):
    hidden_parts = refs[:pieces]
    grads, own, send, totals, hidden, sems = refs[pieces:]
    step = pl.program_id(0)
    segments = totals.shape[0] - 1
    width = weights.shape[-1]
    share = own.shape[0]

    @pl.when(step == 0)
    def _():
        copies = []
        start = 0
        for number, part in enumerate(hidden_parts):
            count = part.shape[0]
            copies.append(
                pltpu.make_async_copy(part, hidden.at[pl.ds(start, count)], sems.at[number])
            )
            copies[-1].start()
            start += count
        totals[...] = jnp.zeros(totals.shape, jnp.float32)
        for copy in copies:
            copy.wait()

    for slot in range(CHUNK):
        k = step * CHUNK + slot
        model = model_at[k]
        values = hidden[hidden_at[k]]
        is_live = live[k] > 0
        term = contract(values, weights[slot], 1, 1 if transposed else 0)
        totals[jnp.where(is_live, model, segments)] += term
        other = lanes(panel, model, width)
        if transposed:
            grad = contract(other, values, 0, 0)
        else:
            grad = contract(values, other, 0, 0)
        grads[slot] = jnp.where(is_live, grad, 0.0).astype(jnp.bfloat16)

    @pl.when(step == pl.num_programs(0) - 1)
    def _():
        for segment in range(segments):
            columns = pl.ds(segment * width, width)
            own[:, columns] = totals[segment, pl.ds(0, share), :]
            for number in range(send.shape[0]):
                rows = pl.ds((number + 1) * share, share)
                send[number, :, columns] = totals[segment, rows, :].astype(jnp.bfloat16)


def to_model(panel, hidden_parts, weights, model_at, hidden_at, live, members, transposed):
    tokens, columns = panel.shape
    slots, width, _ = weights.shape
    segments = columns // width
    share = tokens // members
    hidden_count = sum(part.shape[0] for part in hidden_parts)
    pieces = len(hidden_parts)
    return pl.pallas_call(
        functools.partial(to_model_kernel, transposed, pieces),
        grid_spec=pltpu.PrefetchScalarGridSpec(
            num_scalar_prefetch=3,
            grid=(slots // CHUNK,),
            in_specs=[
                pl.BlockSpec(panel.shape, lambda s, a, b, c: (0, 0)),
                pl.BlockSpec((CHUNK, width, width), lambda s, a, b, c: (s, 0, 0)),
            ]
            + [pl.BlockSpec(memory_space=pl.ANY)] * pieces,
            out_specs=[
                pl.BlockSpec((CHUNK, width, width), lambda s, a, b, c: (s, 0, 0)),
                pl.BlockSpec((share, columns), lambda s, a, b, c: (0, 0)),
                pl.BlockSpec((members - 1, share, columns), lambda s, a, b, c: (0, 0, 0)),
            ],
            scratch_shapes=[
                pltpu.VMEM((segments + 1, tokens, width), jnp.float32),
                pltpu.VMEM((hidden_count, tokens, width), jnp.bfloat16),
                pltpu.SemaphoreType.DMA((pieces,)),
            ],
        ),
        out_shape=[
            jax.ShapeDtypeStruct(weights.shape, jnp.bfloat16),
            jax.ShapeDtypeStruct((share, columns), jnp.float32),
            jax.ShapeDtypeStruct((members - 1, share, columns), jnp.bfloat16),
        ],
        compiler_params=pltpu.CompilerParams(vmem_limit_bytes=VMEM_LIMIT),
        cost_estimate=pl.CostEstimate(
            flops=16 * slots * tokens * width * width,
            bytes_accessed=4 * weights.size + 2 * hidden_count * tokens * width,
            transcendentals=0,
        ),
    )(model_at, hidden_at, live, panel, weights, *hidden_parts)


def swap(values, bit):
    count = lax.axis_size("row")
    return lax.ppermute(values, "row", [(s, s ^ (1 << bit)) for s in range(count)])


def swap_orders():
    rest = list(range(1, int(math.log2(lax.axis_size("row")))))
    return [rest, rest[::-1]]


def hidden_position(index, segments):
    level = int(math.log2(segments))
    row = lax.axis_index("row")
    masks = []
    for order in swap_orders():
        mask = (row & 1) << (level - 1)
        for number, bit in enumerate(order):
            mask = mask | (((row >> bit) & 1) << (level - 3 - number))
        masks.append(mask)
    is_late = ((index >> (level - 2)) & 1) > 0
    return index ^ jnp.where(is_late, masks[1], masks[0])


def scatter_sum(keep, send):
    total = keep + swap(send, 0).astype(jnp.float32)
    quarter = total.shape[0] // 2
    parts = []
    for number, order in enumerate(swap_orders()):
        part = total[number * quarter : (number + 1) * quarter]
        for bit in order:
            half = part.shape[0] // 2
            arrived = swap(part[half:].astype(jnp.bfloat16), bit)
            part = part[:half] + arrived.astype(jnp.float32)
        parts.append(part)
    return parts


def gather_parts(parts):
    near, far = [], []
    for part, order in zip(parts, swap_orders()):
        stages = order[::-1]
        for bit in stages[:-1]:
            part = jnp.concatenate([part, swap(part, bit)], axis=0)
        pair = [part, swap(part, stages[-1])]
        near += pair
        far += [swap(piece, 0) for piece in pair]
    return near + far


def shift(values, distance):
    count = lax.axis_size("col")
    return lax.ppermute(values, "col", [(s, (s + distance) % count) for s in range(count)])


def gather_tokens(values):
    count = lax.axis_size("col")
    return jnp.concatenate([values] + [shift(values, -d) for d in range(1, count)], axis=0)


def scatter_tokens(own, send):
    total = own
    for number in range(send.shape[0]):
        total = total + shift(send[number], number + 1).astype(jnp.float32)
    return total


def body(activations, grad_out, first_blocks, first_coords, second_blocks, second_coords):
    width = first_blocks.shape[-1]
    members = lax.axis_size("col")
    row_tiles = activations.shape[1] // width
    col_tiles = FF // width // members
    row_base = lax.axis_index("row") * row_tiles
    col_base = lax.axis_index("col") * col_tiles

    def fields(model, hidden):
        is_live = model >= 0
        model_at = jnp.where(is_live, model - row_base, 0)
        hidden_at = jnp.where(is_live, hidden_position(hidden - col_base, col_tiles), 0)
        target = jnp.where(is_live, hidden_at, col_tiles)
        return model_at, hidden_at, target, is_live.astype(jnp.int32)

    model_one, hidden_one, target_one, live_one = fields(
        first_coords[0, 0, :, 0], first_coords[0, 0, :, 1]
    )
    model_two, hidden_two, target_two, live_two = fields(
        second_coords[0, 0, :, 1], second_coords[0, 0, :, 0]
    )
    weights_one = first_blocks[0, 0]
    weights_two = second_blocks[0, 0]

    inputs_all = gather_tokens(activations)
    cotangent_all = gather_tokens(grad_out)
    pre_parts = scatter_sum(
        *to_hidden(inputs_all, weights_one, model_one, target_one, col_tiles, False)
    )
    back_parts = scatter_sum(
        *to_hidden(cotangent_all, weights_two, model_two, target_two, col_tiles, True)
    )
    hidden_own, grad_pre_own = [], []
    for pre, back in zip(pre_parts, back_parts):
        hidden_full, gelu_back = jax.vjp(gelu_tanh, pre)
        hidden_own.append(hidden_full.astype(jnp.bfloat16))
        grad_pre_own.append(gelu_back(back)[0].astype(jnp.bfloat16))
    hidden_parts = gather_parts(hidden_own)
    grad_pre_parts = gather_parts(grad_pre_own)
    grad_second, own_out, send_out = to_model(
        cotangent_all, hidden_parts, weights_two, model_two, hidden_two, live_two, members, False
    )
    output = scatter_tokens(own_out, send_out)
    grad_first, own_in, send_in = to_model(
        inputs_all, grad_pre_parts, weights_one, model_one, hidden_one, live_one, members, True
    )
    grad_input = scatter_tokens(own_in, send_in)
    return (output, grad_input, grad_first[None, None], grad_second[None, None])


def solution(mesh):
    return jax.shard_map(
        body,
        mesh=mesh,
        in_specs=(
            P("col", "row"),
            P("col", "row"),
            P("row", "col", None, None, None),
            P("row", "col", None, None),
            P("col", "row", None, None, None),
            P("col", "row", None, None),
        ),
        out_specs=(
            P("col", "row"),
            P("col", "row"),
            P("row", "col", None, None, None),
            P("col", "row", None, None, None),
        ),
        check_vma=False,
    )
```

```python
import functools
import math

import jax
import jax.numpy as jnp
from jax import lax
from jax.experimental import pallas as pl
from jax.experimental.pallas import tpu as pltpu
from jax.sharding import PartitionSpec as P

FF = 65536
CHUNK = 32
VMEM_LIMIT = 58 * 1024 * 1024


def gelu_tanh(values):
    return jax.nn.gelu(values, approximate=True)


def contract(left, right, left_dim, right_dim):
    return lax.dot_general(
        left, right, (((left_dim,), (right_dim,)), ((), ())), preferred_element_type=jnp.float32
    )


def lanes(ref, index, width):
    return ref[:, pl.ds(pl.multiple_of(index * width, width), width)]


def to_hidden_kernel(flipped, source, target, panel, weights, keep, send, totals):
    step = pl.program_id(0)
    segments = totals.shape[0] - 1
    half = segments // 2
    width = weights.shape[-1]

    @pl.when(step == 0)
    def _():
        def clear(index, carry):
            totals[index] = jnp.zeros(totals.shape[1:], jnp.float32)
            return carry

        lax.fori_loop(0, segments, clear, 0)

    for slot in range(CHUNK):
        k = step * CHUNK + slot
        term = contract(
            lanes(panel, source[k], width), weights[slot], 1, 1 if flipped else 0
        )
        totals[target[k]] += term

    @pl.when(step == pl.num_programs(0) - 1)
    def _():
        def write(index, carry):
            keep[index] = totals[index]
            send[index] = totals[half + index].astype(jnp.bfloat16)
            return carry

        lax.fori_loop(0, half, write, 0)


def to_hidden(panel, weights, source, target, segments, flipped):
    tokens = panel.shape[0]
    slots, width, _ = weights.shape
    half = segments // 2
    return pl.pallas_call(
        functools.partial(to_hidden_kernel, flipped),
        grid_spec=pltpu.PrefetchScalarGridSpec(
            num_scalar_prefetch=2,
            grid=(slots // CHUNK,),
            in_specs=[
                pl.BlockSpec(panel.shape, lambda s, a, b: (0, 0)),
                pl.BlockSpec((CHUNK, width, width), lambda s, a, b: (s, 0, 0)),
            ],
            out_specs=[pl.BlockSpec((half, tokens, width), lambda s, a, b: (0, 0, 0))] * 2,
            scratch_shapes=[pltpu.VMEM((segments + 1, tokens, width), jnp.float32)],
        ),
        out_shape=[
            jax.ShapeDtypeStruct((half, tokens, width), jnp.float32),
            jax.ShapeDtypeStruct((half, tokens, width), jnp.bfloat16),
        ],
        compiler_params=pltpu.CompilerParams(vmem_limit_bytes=VMEM_LIMIT),
        cost_estimate=pl.CostEstimate(
            flops=8 * slots * tokens * width * width,
            bytes_accessed=2 * weights.size + 6 * half * tokens * width,
            transcendentals=0,
        ),
    )(source, target, panel, weights)


def fetch(parts, hidden, sems):
    copies = []
    start = 0
    for number, part in enumerate(parts):
        count = part.shape[0]
        copies.append(pltpu.make_async_copy(part, hidden.at[pl.ds(start, count)], sems.at[number]))
        copies[-1].start()
        start += count
    for copy in copies:
        copy.wait()


def to_model_kernel(transposed, pieces, with_sums, with_grads, model_at, hidden_at, live, *refs):
    refs = list(refs)
    panel = refs.pop(0) if with_grads else None
    weights = refs.pop(0) if with_sums else None
    hidden_parts = [refs.pop(0) for _ in range(pieces)]
    grads = refs.pop(0) if with_grads else None
    own, send, totals = [refs.pop(0) for _ in range(3)] if with_sums else (None, None, None)
    hidden, sems = refs
    step = pl.program_id(0)
    width = hidden.shape[-1]

    @pl.when(step == 0)
    def _():
        if with_sums:
            totals[...] = jnp.zeros(totals.shape, jnp.float32)
        fetch(hidden_parts, hidden, sems)

    for slot in range(CHUNK):
        k = step * CHUNK + slot
        model = model_at[k]
        values = hidden[hidden_at[k]]
        is_live = live[k] > 0
        if with_sums:
            term = contract(values, weights[slot], 1, 1 if transposed else 0)
            totals[jnp.where(is_live, model, totals.shape[0] - 1)] += term
        if with_grads:
            other = lanes(panel, model, width)
            if transposed:
                grad = contract(other, values, 0, 0)
            else:
                grad = contract(values, other, 0, 0)
            grads[slot] = jnp.where(is_live, grad, 0.0).astype(jnp.bfloat16)

    if with_sums:

        @pl.when(step == pl.num_programs(0) - 1)
        def _():
            share = own.shape[0]
            for segment in range(totals.shape[0] - 1):
                columns = pl.ds(segment * width, width)
                own[:, columns] = totals[segment, pl.ds(0, share), :]
                for number, piece in enumerate(send):
                    rows = pl.ds((number + 1) * share, share)
                    piece[:, columns] = totals[segment, rows, :].astype(jnp.bfloat16)


def to_model(
    panel, hidden_parts, weights, places, members, transposed, with_sums=True, with_grads=True
):
    tokens, columns = panel.shape
    slots, width, _ = weights.shape
    segments = columns // width
    share = tokens // members
    hidden_count = sum(part.shape[0] for part in hidden_parts)
    pieces = len(hidden_parts)
    chunk_spec = pl.BlockSpec((CHUNK, width, width), lambda s, a, b, c: (s, 0, 0))
    share_spec = pl.BlockSpec((share, columns), lambda s, a, b, c: (0, 0))
    operands, in_specs, out_specs, out_shape, scratch = [], [], [], [], []
    if with_grads:
        operands.append(panel)
        in_specs.append(pl.BlockSpec(panel.shape, lambda s, a, b, c: (0, 0)))
        out_specs.append(chunk_spec)
        out_shape.append(jax.ShapeDtypeStruct(weights.shape, jnp.bfloat16))
    if with_sums:
        operands.append(weights)
        in_specs.append(chunk_spec)
        out_specs += [share_spec, [share_spec] * (members - 1)]
        out_shape += [
            jax.ShapeDtypeStruct((share, columns), jnp.float32),
            [jax.ShapeDtypeStruct((share, columns), jnp.bfloat16)] * (members - 1),
        ]
        scratch.append(pltpu.VMEM((segments + 1, tokens, width), jnp.float32))
    scratch += [
        pltpu.VMEM((hidden_count, tokens, width), jnp.bfloat16),
        pltpu.SemaphoreType.DMA((pieces,)),
    ]

    def kernel(*refs):
        flat = list(refs)
        if with_sums:
            start = 3 + len(operands) + pieces + (1 if with_grads else 0) + 1
            if not isinstance(flat[start], (list, tuple)):
                flat[start : start + members - 1] = [flat[start : start + members - 1]]
        to_model_kernel(transposed, pieces, with_sums, with_grads, *flat)

    return pl.pallas_call(
        kernel,
        grid_spec=pltpu.PrefetchScalarGridSpec(
            num_scalar_prefetch=3,
            grid=(slots // CHUNK,),
            in_specs=in_specs + [pl.BlockSpec(memory_space=pl.ANY)] * pieces,
            out_specs=out_specs,
            scratch_shapes=scratch,
        ),
        out_shape=out_shape,
        compiler_params=pltpu.CompilerParams(vmem_limit_bytes=VMEM_LIMIT),
        cost_estimate=pl.CostEstimate(
            flops=8 * slots * tokens * width * width * (with_sums + with_grads),
            bytes_accessed=4 * weights.size + 2 * hidden_count * tokens * width,
            transcendentals=0,
        ),
    )(*places, *operands, *hidden_parts)


def swap(values, bit):
    count = lax.axis_size("row")
    return lax.ppermute(values, "row", [(s, s ^ (1 << bit)) for s in range(count)])


def swap_orders():
    rest = list(range(1, int(math.log2(lax.axis_size("row")))))
    return [rest, rest[::-1]]


def hidden_position(index, segments):
    level = int(math.log2(segments))
    row = lax.axis_index("row")
    masks = []
    for order in swap_orders():
        mask = (row & 1) << (level - 1)
        for number, bit in enumerate(order):
            mask = mask | (((row >> bit) & 1) << (level - 3 - number))
        masks.append(mask)
    is_late = ((index >> (level - 2)) & 1) > 0
    return index ^ jnp.where(is_late, masks[1], masks[0])


def after(values, *earlier):
    return lax.optimization_barrier((values, earlier))[0]


def added(terms, start, count):
    total = None
    for array, base in terms:
        piece = array[base + start : base + start + count].astype(jnp.float32)
        total = piece if total is None else total + piece
    return total


def scatter_begin(keep, send):
    arrived = swap(send, 0)
    quarter = keep.shape[0] // 2
    half = quarter // 2
    parts = [[(keep, n * quarter), (arrived, n * quarter)] for n in range(2)]
    sent = [added(terms, half, half).astype(jnp.bfloat16) for terms in parts]
    return parts, sent, [swap(v, order[0]) for v, order in zip(sent, swap_orders())]


def scatter_end(parts, arrived):
    results = []
    for terms, first, order in zip(parts, arrived, swap_orders()):
        terms = terms + [(first, 0)]
        half = first.shape[0]
        for bit in order[1:]:
            half = half // 2
            terms.append((swap(added(terms, half, half).astype(jnp.bfloat16), bit), 0))
        results.append(added(terms, 0, half))
    return results


def gather_near(parts):
    pairs = []
    for part, order in zip(parts, swap_orders()):
        stages = order[::-1]
        for bit in stages[:-1]:
            part = jnp.concatenate([part, swap(part, bit)], axis=0)
        pairs.append((part, swap(part, stages[-1])))
    return pairs


def gather_far(pairs, *earlier):
    far = []
    for first, second in pairs:
        late = after(second, *earlier) if earlier else second
        far += [swap(first, 0), swap(late, 0)]
    return [piece for pair in pairs for piece in pair] + far


def shift(values, distance):
    count = lax.axis_size("col")
    return lax.ppermute(values, "col", [(s, (s + distance) % count) for s in range(count)])


def gather_tokens(values):
    count = lax.axis_size("col")
    return jnp.concatenate([values] + [shift(values, -d) for d in range(1, count)], axis=0)


def scatter_tokens(own, send):
    total = own
    for number, piece in enumerate(send):
        total = total + shift(piece, number + 1).astype(jnp.float32)
    return total


def body(activations, grad_out, first_blocks, first_coords, second_blocks, second_coords):
    width = first_blocks.shape[-1]
    members = lax.axis_size("col")
    row_tiles = activations.shape[1] // width
    col_tiles = FF // width // members
    row_base = lax.axis_index("row") * row_tiles
    col_base = lax.axis_index("col") * col_tiles

    def fields(model, hidden):
        is_live = model >= 0
        model_at = jnp.where(is_live, model - row_base, 0)
        hidden_at = jnp.where(is_live, hidden_position(hidden - col_base, col_tiles), 0)
        target = jnp.where(is_live, hidden_at, col_tiles)
        return model_at, hidden_at, target, is_live.astype(jnp.int32)

    model_one, hidden_one, target_one, live_one = fields(
        first_coords[0, 0, :, 0], first_coords[0, 0, :, 1]
    )
    model_two, hidden_two, target_two, live_two = fields(
        second_coords[0, 0, :, 1], second_coords[0, 0, :, 0]
    )
    weights_one = first_blocks[0, 0]
    weights_two = second_blocks[0, 0]

    inputs_all = gather_tokens(activations)
    cotangent_all = gather_tokens(after(grad_out, inputs_all))
    pre_keep, pre_send = to_hidden(
        inputs_all, weights_one, model_one, target_one, col_tiles, False
    )
    pre_terms, pre_sent, pre_arrived = scatter_begin(pre_keep, after(pre_send, cotangent_all))
    back_keep, back_send = to_hidden(
        after(cotangent_all, *pre_sent), weights_two, model_two, target_two, col_tiles, True
    )
    back_terms, _, back_arrived = scatter_begin(back_keep, after(back_send, *pre_arrived))
    pre_parts = scatter_end(pre_terms, pre_arrived)
    back_parts = scatter_end(back_terms, back_arrived)
    hidden_own, grad_pre_own = [], []
    for pre, back in zip(pre_parts, back_parts):
        hidden_full, gelu_back = jax.vjp(gelu_tanh, pre)
        hidden_own.append(hidden_full.astype(jnp.bfloat16))
        grad_pre_own.append(gelu_back(back)[0].astype(jnp.bfloat16))
    hidden_near = gather_near(hidden_own)
    hidden_parts = gather_far(hidden_near)
    grad_pre_near = gather_near(after(grad_pre_own, *hidden_near))
    grad_second, own_out, send_out = to_model(
        cotangent_all, hidden_parts, weights_two, (model_two, hidden_two, live_two), members, False
    )
    grad_pre_parts = gather_far(grad_pre_near, own_out)
    output = scatter_tokens(own_out, after(send_out, *grad_pre_parts))
    places_one = (model_one, hidden_one, live_one)
    own_in, send_in = to_model(
        inputs_all,
        grad_pre_parts,
        weights_one,
        places_one,
        members,
        True,
        with_grads=False,
    )
    grad_input = scatter_tokens(own_in, send_in)
    (grad_first,) = to_model(
        inputs_all,
        after(grad_pre_parts, own_in, output),
        weights_one,
        places_one,
        members,
        True,
        with_sums=False,
    )
    return (output, grad_input, grad_first[None, None], grad_second[None, None])


def solution(mesh):
    return jax.shard_map(
        body,
        mesh=mesh,
        in_specs=(
            P("col", "row"),
            P("col", "row"),
            P("row", "col", None, None, None),
            P("row", "col", None, None),
            P("col", "row", None, None, None),
            P("col", "row", None, None),
        ),
        out_specs=(
            P("col", "row"),
            P("col", "row"),
            P("row", "col", None, None, None),
            P("col", "row", None, None, None),
        ),
        check_vma=False,
    )
```
